32 devices in a mesh: dp: 8 (over z, core), expert: 4 (over y, x).
Axes of the slice: x: 2, y: 2, z: 4, core: 2. Of those that a mesh axis runs over, the one named last changes fastest.
Arguments:
- tokens: bfloat16 [4096, 2048], P(('dp', 'expert')), may hold values from -6 to 6
- upstream: bfloat16 [4096, 2048], P(('dp', 'expert')), may hold values from -6 to 6
- expert_ids: int32 [4096, 8], P(('dp', 'expert')), may hold values from 0 to 31, all different within a row; in each aligned block of 128 rows (0 to 127, 128 to 255, ...) at most 40 rows name the same one
- gate_weights: bfloat16 [4096, 8], P(('dp', 'expert')), may hold values from 0.049804688 to 0.5
- w_up: bfloat16 [4, 2048, 768], P('expert'), may hold values from -0.125 to 0.125
- w_down: bfloat16 [4, 768, 2048], P('expert'), may hold values from -0.21875 to 0.21875
Outputs:
- token_grads: bfloat16 [4096, 2048], P(('dp', 'expert'))
- gate_grads: bfloat16 [4096, 8], P(('dp', 'expert'))
- router_grads: float32 [4, 2048], P('expert')
The draws below stay inside these ranges and needn't reach their ends.
Inputs may be any that keep to these rules, and one draw needn't show every extreme that they name: `expert_ids`: each row names 8 different experts; among the 128 rows of one device no expert is named by more than 40 rows.
All inputs are finite; a program needn't handle non-finite values.
Results may differ from the reference program's by a relative error of at most 0.0063.
Values may be sent and summed in bfloat16 or wider, within the bound.
A program may use at most 64 MiB of HBM per device.

```python
import math
import jax
import jax.numpy as jnp
import numpy as np
from jax import lax

D = 2048
F = 768
TOP = 8
EXP_DEV = 8
TOK_DEV = 128
EXPERTS = 32
FLIGHTS = 4
MOST = 40
COLUMN_TOK = 1024
TOKENS = 4096
N_DP = 8
N_EXPERT = 4


def block_levels(rng, dims, cuts, low, top_value):
    loudness = 1.0
    for dim, shards_of in cuts:
        draws = jax.random.uniform(jax.random.fold_in(jax.random.fold_in(rng, 6), dim), (shards_of,), jnp.float32, low / len(cuts), top_value / len(cuts))
        loudness = loudness * jnp.repeat(jnp.exp(draws), dims[dim] // shards_of).reshape((-1,) + (1,) * (len(dims) - 1 - dim))
    return loudness


def shared_out(key, own, number, rows, amount, top, bound, slope):
    ranking = jax.random.permutation(key, amount)
    crowded, usual = portions_of(amount, rows * top, bound, slope, True), portions_of(amount, rows * top, bound, slope, False)
    places = jnp.arange(amount)

    def named(tallies, offset_by):
        used = int((tallies > 0).sum())
        fixed = max(1, used // 4)
        passed = fixed + (places - fixed + offset_by * (used - fixed)) % max(1, amount - fixed)
        return jnp.zeros((amount,), jnp.int32).at[ranking[jnp.where(places < fixed, places, passed)]].set(jnp.asarray(tallies, jnp.int32))

    tallies = jnp.where(number % 4 == 0, named(crowded, number // 4), named(usual, number - number // 4 - 1))
    mixed = jax.random.permutation(jax.random.fold_in(own, 3), amount)
    source_of, sink = mixed[0:amount // 2 * 2:2], mixed[1:amount // 2 * 2:2]
    margin = jnp.minimum(tallies[source_of] - 1, bound - tallies[sink]) // 2
    margin = jnp.where((source_of == ranking[0]) | (sink == ranking[0]) | (tallies[sink] == 0), 0, jnp.maximum(margin, 0))
    passed = jax.random.randint(jax.random.fold_in(own, 4), (amount // 2,), 0, 1 << 20) % (margin + 1)
    tallies = tallies.at[source_of].add(-passed).at[sink].add(passed)
    members = jnp.searchsorted(jnp.cumsum(tallies), jnp.arange(rows * top), side="right").astype(jnp.int32)
    listing = members.reshape(top, rows).T
    listing = listing[jax.random.permutation(jax.random.fold_in(own, 1), rows)]
    offset_by = jax.random.randint(jax.random.fold_in(own, 2), (rows, 1), 0, top)
    return jnp.take_along_axis(listing, (jnp.arange(top)[None, :] + offset_by) % top, axis=1)


def portions_of(amount, total, most, slope, full):
    portions = [(1 << 20) // math.isqrt(rank ** slope) + 1 for rank in range(1, amount + 1)]
    largest = most if full else min(most, max(-(-total // amount), total * portions[0] // sum(portions)))
    least = 1 if total - largest >= amount - 1 else 0
    given, surplus = [largest] + [least] * (amount - 1), total - largest - least * (amount - 1)
    while surplus > 0:
        free = [i for i in range(1, amount) if given[i] < largest] or [i for i in range(1, amount) if given[i] < most]
        pool, left = sum([portions[i] for i in free]), surplus
        for i in free:
            extra = min(most - given[i], max(1, left * portions[i] // pool), surplus)
            given[i] = given[i] + extra
            surplus = surplus - extra
    return np.array(given)


def noise(rng, extent, scale, bound, shards=(), held_as=jnp.bfloat16):
    values = scale * jax.random.normal(rng, extent, jnp.float32)
    if shards:
        values = values * block_levels(rng, extent, shards, -0.22, 0.18)
    return jnp.clip(values, -bound, bound).astype(held_as)


def setup_inputs(seed: int = 0) -> dict:
    key_of = jax.random.split(jax.random.key(seed), 7)
    tokens = noise(key_of[0], (TOKENS, D), 1.0, 6.0, ((0, 32),))
    upstream = noise(key_of[1], (TOKENS, D), 1.0, 6.0, ((0, 32),))
    expert_ids_keys = jax.random.split(jax.random.fold_in(key_of[2], 1), TOKENS // TOK_DEV)
    expert_ids_turns = jax.random.permutation(jax.random.fold_in(key_of[2], 3), TOKENS // TOK_DEV)
    expert_ids = jax.vmap(lambda own, number: shared_out(jax.random.fold_in(key_of[2], 2), own, number, TOK_DEV, EXPERTS, TOP, MOST, 2))(expert_ids_keys, expert_ids_turns).reshape((TOKENS, TOP))
    gate_weights = jnp.clip(0.049804688 + 0.4501953 * jax.random.uniform(key_of[3], (TOKENS, TOP), jnp.float32) ** block_levels(key_of[3], (TOKENS, TOP), ((0, 32),), -0.2, 0.2), 0.049804688, 0.5).astype(jnp.bfloat16)
    w_up = noise(key_of[4], (FLIGHTS, D, F), D ** -0.5, 0.125, ((0, 4),))
    w_down = noise(key_of[5], (FLIGHTS, F, D), F ** -0.5, 0.21875, ((0, 4),))
    return dict(tokens=tokens, upstream=upstream, expert_ids=expert_ids, gate_weights=gate_weights, w_up=w_up, w_down=w_down)


def reference(tokens, upstream, expert_ids, gate_weights, w_up, w_down):
    flat_ids = expert_ids.reshape(-1)
    flat_gates = gate_weights.reshape(-1)
    live = (flat_ids % EXP_DEV) == 0
    limit = N_DP * N_EXPERT * MOST

    def one_expert(index):
        hit = live & ((flat_ids // EXP_DEV) == index)
        places = jnp.nonzero(hit, size=limit, fill_value=0)[0].astype(jnp.int32)
        valid = jnp.arange(limit) < jnp.sum(hit.astype(jnp.int32))
        owners = (places // TOP).astype(jnp.int32)
        rows_x = tokens[owners]
        rows_dy = upstream[owners]
        rows_gate = jnp.where(valid, flat_gates[places].astype(jnp.float32), 0.0)
        up_mat = w_up[index]
        down_mat = w_down[index]
        act = jnp.dot(rows_x, up_mat, preferred_element_type=jnp.float32)
        sig = jax.nn.sigmoid(act)
        hidden = (act * sig).astype(jnp.bfloat16)
        expert_out = jnp.dot(hidden, down_mat, preferred_element_type=jnp.float32)
        gate_term = jnp.sum(rows_dy.astype(jnp.float32) * expert_out, axis=1)
        gate_term = jnp.where(valid, gate_term, 0.0)
        router_col = jnp.sum(gate_term[:, None] * rows_x.astype(jnp.float32), axis=0)
        scaled = (rows_gate[:, None] * rows_dy.astype(jnp.float32)).astype(jnp.bfloat16)
        back = lax.dot_general(scaled, down_mat, (((1,), (1,)), ((), ())), preferred_element_type=jnp.float32)
        act_grad = (back * sig * (1.0 + act * (1.0 - sig))).astype(jnp.bfloat16)
        route_grad = lax.dot_general(act_grad, up_mat, (((1,), (1,)), ((), ())), preferred_element_type=jnp.float32).astype(jnp.bfloat16)
        return route_grad, gate_term, router_col, places, valid

    route_grad, gate_term, router_cols, places, valid = lax.map(one_expert, jnp.arange(N_EXPERT))
    owners = (places // TOP).astype(jnp.int32).reshape(-1)
    terms = jnp.where(valid.reshape(-1)[:, None], route_grad.reshape(-1, D).astype(jnp.float32), 0.0)
    token_grads = jnp.zeros((TOKENS, D), jnp.float32).at[owners].add(terms).astype(jnp.bfloat16)
    gate_vals = gate_term.astype(jnp.bfloat16).astype(jnp.float32)
    gate_flat = jnp.zeros((TOKENS * TOP,), jnp.float32).at[places.reshape(-1)].add(jnp.where(valid, gate_vals, 0.0).reshape(-1))
    gate_grads = gate_flat.reshape(TOKENS, TOP).astype(jnp.bfloat16)
    router_grads = router_cols / jnp.float32(COLUMN_TOK)
    return token_grads, gate_grads, router_grads
```

```python
import functools
import jax
import jax.numpy as jnp
from jax import lax
from jax.experimental import pallas as pl
from jax.experimental.pallas import tpu as pltpu
from jax.sharding import PartitionSpec as P

EXP_DEV = 8
MESH = pl.DeviceIdType.MESH
F32 = jnp.float32
BF16 = jnp.bfloat16


def nt_dot(a, b):
    return lax.dot_general(a, b, (((1,), (1,)), ((), ())), preferred_element_type=F32)


def flipped(me, j):
    out, bit = me, 1
    while bit <= j:
        if (j // bit) % 2:
            out = out + bit - 2 * bit * ((me // bit) % 2)
        bit *= 2
    return out


def kernel(n, dp, rows, groups, tok_hbm, dy_hbm, ids_ref, gate_ref, wu_hbm, wd_hbm,
           tg_ref, gg_ref, rg_ref,
           tok, dy, wu, wd, send, recv, rsend, rrecv, gsend, grecv, agr, cols, gl, gr,
           local_sem, s_send, s_recv, r_send, r_recv, g_send, g_recv, c_send, c_recv):
    me = lax.axis_index("expert")
    my_dp = lax.axis_index("dp")
    tok_count, width = tok.shape
    hidden = wu.shape[1]
    top = ids_ref.shape[1]
    half = width // 2
    hi = -(-rows // 16) * 16
    lo = rows // 16 * 16
    off = rows - lo
    span = 2 * rows - lo
    peers = [flipped(me, j) for j in range(n)]

    loads = [
        pltpu.make_async_copy(src, dst, local_sem.at[i])
        for i, (src, dst) in enumerate(
            ((tok_hbm, tok), (dy_hbm, dy), (wu_hbm, wu), (wd_hbm, wd)))
    ]
    for load in loads:
        load.start()

    barrier = pltpu.get_barrier_semaphore()
    for j in range(1, n):
        pl.semaphore_signal(barrier, inc=1, device_id=(my_dp, peers[j]), device_id_type=MESH)
    for k in range(1, dp):
        pl.semaphore_signal(
            barrier, inc=1, device_id=(lax.rem(my_dp + k, dp), me), device_id_type=MESH)

    ids = ids_ref[...]
    gates = gate_ref[...].astype(F32)
    lane = lax.broadcasted_iota(jnp.int32, (1, 128), 1)
    target = jnp.full((1, 128), -1, jnp.int32)
    for j in range(n):
        target = jnp.where(lane == j, EXP_DEV * peers[j], target)
    hit = jnp.zeros((tok_count, 128), F32)
    gsel = jnp.zeros((tok_count, 128), F32)
    for k in range(top):
        same = ids[:, k:k + 1] == target
        hit = hit + jnp.where(same, 1.0, 0.0)
        gsel = gsel + jnp.where(same, gates[:, k:k + 1], 0.0)
    t_row = lax.broadcasted_iota(jnp.int32, (tok_count, tok_count), 0)
    t_col = lax.broadcasted_iota(jnp.int32, (tok_count, tok_count), 1)
    below = jnp.where(t_col < t_row, 1.0, 0.0).astype(BF16)
    eye = jnp.where(t_col == t_row, 1.0, 0.0).astype(BF16)
    rank = jnp.dot(below, hit.astype(BF16), preferred_element_type=F32)
    key = jnp.where(hit > 0.5, rank, -1.0)
    key_t = lax.dot_general(
        key.astype(BF16), eye, (((0,), (0,)), ((), ())), preferred_element_type=F32)

    row_id = lax.broadcasted_iota(jnp.int32, (rows, tok_count), 0).astype(F32)
    picks = [
        jnp.where(row_id == key_t[j:j + 1, :], 1.0, 0.0)
        for j in range(n)
    ]
    pick_all = jnp.concatenate(picks, axis=0).astype(BF16)
    loads[0].wait()
    loads[1].wait()
    for c in range(0, width, 512):
        sel_x = jnp.dot(pick_all, tok[:, c:c + 512], preferred_element_type=F32)
        sel_d = jnp.dot(pick_all, dy[:, c:c + 512], preferred_element_type=F32)
        for j in range(n):
            both = jnp.concatenate(
                [sel_x[j * rows:(j + 1) * rows], sel_d[j * rows:(j + 1) * rows]], axis=0)
            if j == 0:
                recv[0, :, c:c + 512] = both.astype(BF16)
            else:
                send[j, :, c:c + 512] = both.astype(BF16)

    pl.semaphore_wait(barrier, n - 1 + dp - 1)

    def remote(src, dst, a_sem, b_sem, j):
        return pltpu.make_async_remote_copy(
            src_ref=src.at[j], dst_ref=dst.at[j], send_sem=a_sem.at[j], recv_sem=b_sem.at[j],
            device_id=(my_dp, peers[j]), device_id_type=MESH)

    out_copies = [None] + [remote(send, recv, s_send, s_recv, j) for j in range(1, n)]
    for j in range(1, n):
        out_copies[j].start()

    lanes = lax.broadcasted_iota(jnp.int32, (1, n * hi), 1).astype(F32)
    mat = jnp.zeros((tok_count, n * hi), F32)
    mat_r = jnp.zeros((tok_count, n * span), F32)
    lanes_r = lax.broadcasted_iota(jnp.int32, (1, n * span), 1).astype(F32)
    for j in range(n):
        there = hit[:, j:j + 1] > 0.5
        spot = jnp.where(there, rank[:, j:j + 1] + (hi * j), -1.0)
        mat = mat + jnp.where(lanes == spot, gsel[:, j:j + 1], 0.0)
        spot_r = jnp.where(there, rank[:, j:j + 1] + (span * j + off), -1.0)
        mat_r = mat_r + jnp.where(lanes_r == spot_r, gsel[:, j:j + 1], 0.0)
    gl[...] = mat.astype(BF16)
    gr[...] = mat_r.astype(BF16)

    loads[2].wait()
    loads[3].wait()
    diag = (lax.broadcasted_iota(jnp.int32, (rows, 128), 0)
            == lax.broadcasted_iota(jnp.int32, (rows, 128), 1))
    total = jnp.zeros((1, width), F32)
    back_copies = []
    for group in groups:
        for j in group:
            if j:
                out_copies[j].wait_recv()
        g = len(group)
        xs = jnp.concatenate([recv[j, 0:hi, :] for j in group], axis=0)
        ds = jnp.concatenate([recv[j, lo:2 * rows, :] for j in group], axis=0)
        terms = [jnp.zeros((rows, 1), F32) for _ in group]
        for c in range(0, hidden, 256):
            act_all = jnp.dot(xs, wu[:, c:c + 256], preferred_element_type=F32)
            u_all = nt_dot(ds, wd[c:c + 256, :])
            grads = []
            for i in range(g):
                act = act_all[i * hi:i * hi + rows]
                u = u_all[i * span + off:i * span + off + rows]
                sig = jax.nn.sigmoid(act)
                hid = (act * sig).astype(BF16).astype(F32)
                terms[i] = terms[i] + jnp.sum(hid * u, axis=1, keepdims=True)
                grads.append(u * sig * (1.0 + act * (1.0 - sig)))
            agr[0:g * rows, c:c + 256] = jnp.concatenate(grads, axis=0).astype(BF16)
        grad_in = agr[0:g * rows, :]
        left = nt_dot(grad_in, wu[0:half, :])
        right = nt_dot(grad_in, wu[half:width, :])
        for i, j in enumerate(group):
            block = jnp.concatenate(
                [left[i * rows:(i + 1) * rows], right[i * rows:(i + 1) * rows]], axis=0)
            line = jnp.sum(jnp.where(diag, terms[i], 0.0), axis=0, keepdims=True)
            line = jnp.broadcast_to(line, (8, 128))
            if j == 0:
                rrecv[0] = block.astype(BF16)
                grecv[0] = line
            else:
                rsend[j] = block.astype(BF16)
                gsend[j] = line
                for args in ((rsend, rrecv, r_send, r_recv), (gsend, grecv, g_send, g_recv)):
                    copy = remote(*args, j)
                    copy.start()
                    back_copies.append(copy)
        for i, j in enumerate(group):
            total = total + jnp.sum(
                recv[j, 0:hi, :].astype(F32)[0:rows] * terms[i], axis=0, keepdims=True)

    cols[my_dp] = total
    col_copies = []
    for k in range(1, dp):
        copy = pltpu.make_async_remote_copy(
            src_ref=cols.at[my_dp], dst_ref=cols.at[my_dp], send_sem=c_send.at[k],
            recv_sem=c_recv.at[k], device_id=(lax.rem(my_dp + k, dp), me), device_id_type=MESH)
        copy.start()
        col_copies.append(copy)

    for k in range(1, dp):
        src = lax.rem(my_dp + dp - k, dp)
        pltpu.make_async_remote_copy(
            src_ref=cols.at[src], dst_ref=cols.at[src], send_sem=c_send.at[k],
            recv_sem=c_recv.at[k], device_id=(src, me), device_id_type=MESH).wait_recv()
    col = cols[0]
    for i in range(1, dp):
        col = col + cols[i]
    rg_ref[...] = col / F32(tok_count * dp)

    for copy in back_copies:
        copy.wait_recv()
    back_l = jnp.concatenate([rrecv[j, 0:hi, :] for j in range(n)], axis=0)
    tg_ref[:, 0:half] = jnp.dot(gl[...], back_l, preferred_element_type=F32).astype(BF16)
    back_r = jnp.concatenate([rrecv[j, lo:2 * rows, :] for j in range(n)], axis=0)
    tg_ref[:, half:width] = jnp.dot(gr[...], back_r, preferred_element_type=F32).astype(BF16)

    gate_out = jnp.zeros((tok_count, top), F32)
    lane_f = lane.astype(F32)
    for j in range(n):
        term = jnp.sum(
            jnp.where(lane_f == key[:, j:j + 1], grecv[j, 0:1, :], 0.0), axis=1, keepdims=True)
        gate_out = gate_out + jnp.where(ids == EXP_DEV * peers[j], term, 0.0)
    gg_ref[...] = gate_out.astype(BF16)

    for copy in out_copies[1:] + back_copies + col_copies:
        copy.wait_send()


def body(tokens, upstream, expert_ids, gate_weights, w_up, w_down):
    n = lax.axis_size("expert")
    dp = lax.axis_size("dp")
    tok_count, width = tokens.shape
    top = expert_ids.shape[1]
    hidden = w_up.shape[2]
    experts = EXP_DEV * n
    most = tok_count * top // experts + tok_count * top // (4 * experts)
    rows = -(-most // 8) * 8
    hi = -(-rows // 16) * 16
    span = 2 * rows - rows // 16 * 16
    groups = [(0,), tuple(range(1, n // 2 + 1)), tuple(range(n // 2 + 1, n))]
    biggest = max(len(g) for g in groups)
    hbm = pl.BlockSpec(memory_space=pl.ANY)
    vmem = pl.BlockSpec(memory_space=pltpu.VMEM)
    dma = pltpu.SemaphoreType.DMA
    return pl.pallas_call(
        functools.partial(kernel, n, dp, rows, groups),
        out_shape=(
            jax.ShapeDtypeStruct((tok_count, width), BF16),
            jax.ShapeDtypeStruct((tok_count, top), BF16),
            jax.ShapeDtypeStruct((1, width), F32),
        ),
        in_specs=[hbm, hbm, vmem, vmem, hbm, hbm],
        out_specs=(vmem, vmem, vmem),
        scratch_shapes=[
            pltpu.VMEM((tok_count, width), BF16),
            pltpu.VMEM((tok_count, width), BF16),
            pltpu.VMEM((width, hidden), BF16),
            pltpu.VMEM((hidden, width), BF16),
            pltpu.VMEM((n, 2 * rows, width), BF16),
            pltpu.VMEM((n, 2 * rows, width), BF16),
            pltpu.VMEM((n, 2 * rows, width // 2), BF16),
            pltpu.VMEM((n, 2 * rows, width // 2), BF16),
            pltpu.VMEM((n, 8, 128), F32),
            pltpu.VMEM((n, 8, 128), F32),
            pltpu.VMEM((-(-biggest * rows // 16) * 16, hidden), BF16),
            pltpu.VMEM((dp, 1, width), F32),
            pltpu.VMEM((tok_count, n * hi), BF16),
            pltpu.VMEM((tok_count, n * span), BF16),
            dma((4,)),
            dma((n,)), dma((n,)), dma((n,)), dma((n,)), dma((n,)), dma((n,)),
            dma((dp,)), dma((dp,)),
        ],
        compiler_params=pltpu.CompilerParams(
            collective_id=0, has_side_effects=True, vmem_limit_bytes=48 * 1024 * 1024),
        cost_estimate=pl.CostEstimate(
            flops=6 * n * rows * width * hidden, bytes_accessed=4 * width * hidden,
            transcendentals=n * rows * hidden),
    )(tokens, upstream, expert_ids, gate_weights, w_up[0], w_down[0])


def solution(mesh):
    return jax.shard_map(
        body,
        mesh=mesh,
        in_specs=(
            P(("dp", "expert"), None),
            P(("dp", "expert"), None),
            P(("dp", "expert"), None),
            P(("dp", "expert"), None),
            P("expert", None, None),
            P("expert", None, None),
        ),
        out_specs=(P(("dp", "expert"), None), P(("dp", "expert"), None), P("expert", None)),
        check_vma=False,
    )
```

```python
import functools
import jax
import jax.numpy as jnp
from jax import lax
from jax.experimental import pallas as pl
from jax.experimental.pallas import tpu as pltpu
from jax.sharding import PartitionSpec as P

EXP_DEV = 8
MESH = pl.DeviceIdType.MESH
F32 = jnp.float32
BF16 = jnp.bfloat16


def nt_dot(a, b):
    return lax.dot_general(a, b, (((1,), (1,)), ((), ())), preferred_element_type=F32)


def flipped(me, j):
    out, bit = me, 1
    while bit <= j:
        if (j // bit) % 2:
            out = out + bit - 2 * bit * ((me // bit) % 2)
        bit *= 2
    return out


def kernel(n, dp, rows, groups, tok_hbm, dy_hbm, ids_ref, gate_ref, wu_hbm, wd_hbm,
           rrecv, gl, gr, gg_ref, rg_ref,
           tok, dy, wu, wd, send, recv, rsend, gsend, grecv, agr, cols, pick,
           local_sem, s_send, s_recv, r_send, r_recv, g_send, g_recv, c_send, c_recv):
    me = lax.axis_index("expert")
    my_dp = lax.axis_index("dp")
    tok_count, width = tok.shape
    hidden = wu.shape[1]
    half = width // 2
    hi = -(-rows // 16) * 16
    lo = rows // 16 * 16
    off = rows - lo
    span = 2 * rows - lo
    peers = [flipped(me, j) for j in range(n)]

    loads = [
        pltpu.make_async_copy(src, dst, local_sem.at[i])
        for i, (src, dst) in enumerate(
            ((tok_hbm, tok), (dy_hbm, dy), (wu_hbm, wu), (wd_hbm, wd)))
    ]
    for load in loads:
        load.start()

    barrier = pltpu.get_barrier_semaphore()
    for j in range(1, n):
        pl.semaphore_signal(barrier, inc=1, device_id=(my_dp, peers[j]), device_id_type=MESH)
    for k in range(1, dp):
        pl.semaphore_signal(
            barrier, inc=1, device_id=(lax.rem(my_dp + k, dp), me), device_id_type=MESH)

    ids = ids_ref[...]
    gates = gate_ref[...].astype(F32)
    hits, gate_rows = [], []
    for j in range(n):
        same = ids == EXP_DEV * peers[j]
        hits.append(jnp.sum(jnp.where(same, 1.0, 0.0), axis=0, keepdims=True))
        gate_rows.append(jnp.sum(jnp.where(same, gates, 0.0), axis=0, keepdims=True))
    pad = [jnp.zeros((128 - n, tok_count), F32)]
    hit_t = jnp.concatenate(hits + pad, axis=0)
    gate_t = jnp.concatenate(gate_rows + pad, axis=0)
    t_row = lax.broadcasted_iota(jnp.int32, (tok_count, tok_count), 0)
    t_col = lax.broadcasted_iota(jnp.int32, (tok_count, tok_count), 1)
    above = jnp.where(t_row < t_col, 1.0, 0.0).astype(BF16)
    eye = jnp.where(t_col == t_row, 1.0, 0.0).astype(BF16)
    rank_t = jnp.dot(hit_t.astype(BF16), above, preferred_element_type=F32)
    key_t = jnp.where(hit_t > 0.5, rank_t, -1.0)

    row_id = lax.broadcasted_iota(jnp.int32, (rows, tok_count), 0).astype(F32)
    for j in range(n):
        pick[j * rows:(j + 1) * rows, :] = jnp.where(row_id == key_t[j:j + 1, :], 1.0, 0.0)
    pick_all = pick[...].astype(BF16)

    def remote(src, dst, a_sem, b_sem, j):
        return pltpu.make_async_remote_copy(
            src_ref=src.at[j], dst_ref=dst.at[j], send_sem=a_sem.at[j], recv_sem=b_sem.at[j],
            device_id=(my_dp, peers[j]), device_id_type=MESH)

    def part(j, h):
        cut = (j, slice(None), pl.ds(h * half, half))
        return pltpu.make_async_remote_copy(
            src_ref=send.at[cut], dst_ref=recv.at[cut], send_sem=s_send.at[2 * j + h],
            recv_sem=s_recv.at[2 * j + h], device_id=(my_dp, peers[j]), device_id_type=MESH)

    out_copies = [[part(j, 0), part(j, 1)] if j else [] for j in range(n)]
    loads[0].wait()
    loads[1].wait()
    for h in range(2):
        for c in range(h * half, h * half + half, 512):
            sel_x = jnp.dot(pick_all, tok[:, c:c + 512], preferred_element_type=F32)
            sel_d = jnp.dot(pick_all, dy[:, c:c + 512], preferred_element_type=F32)
            for j in range(n):
                both = jnp.concatenate(
                    [sel_x[j * rows:(j + 1) * rows], sel_d[j * rows:(j + 1) * rows]], axis=0)
                if j == 0:
                    recv[0, :, c:c + 512] = both.astype(BF16)
                else:
                    send[j, :, c:c + 512] = both.astype(BF16)
        if h == 0:
            pl.semaphore_wait(barrier, n - 1 + dp - 1)
        for j in groups[1]:
            out_copies[j][h].start()

    key = lax.dot_general(
        eye, key_t.astype(BF16), (((1,), (1,)), ((), ())), preferred_element_type=F32)
    gsel = lax.dot_general(
        eye, gate_t.astype(BF16), (((1,), (1,)), ((), ())), preferred_element_type=F32)
    lanes = lax.broadcasted_iota(jnp.int32, (1, n * hi), 1).astype(F32)
    mat = jnp.zeros((tok_count, n * hi), F32)
    mat_r = jnp.zeros((tok_count, n * span), F32)
    lanes_r = lax.broadcasted_iota(jnp.int32, (1, n * span), 1).astype(F32)
    for j in range(n):
        there = key[:, j:j + 1] > -0.5
        spot = jnp.where(there, key[:, j:j + 1] + (hi * j), -1.0)
        mat = mat + jnp.where(lanes == spot, gsel[:, j:j + 1], 0.0)
        spot_r = jnp.where(there, key[:, j:j + 1] + (span * j + off), -1.0)
        mat_r = mat_r + jnp.where(lanes_r == spot_r, gsel[:, j:j + 1], 0.0)
    gl[...] = mat.astype(BF16)
    gr[...] = mat_r.astype(BF16)

    diag = (lax.broadcasted_iota(jnp.int32, (rows, 128), 0)
            == lax.broadcasted_iota(jnp.int32, (rows, 128), 1))
    loads[2].wait()
    loads[3].wait()
    total = jnp.zeros((1, width), F32)
    back_copies, gate_copies = [], []
    for number, group in enumerate(groups):
        for j in group:
            for copy in out_copies[j]:
                copy.wait_recv()
        g = len(group)
        xs = jnp.concatenate([recv[j, 0:hi, :] for j in group], axis=0)
        ds = jnp.concatenate([recv[j, lo:2 * rows, :] for j in group], axis=0)
        terms = [jnp.zeros((rows, 1), F32) for _ in group]
        for c in range(0, hidden, 256):
            act_all = jnp.dot(xs, wu[:, c:c + 256], preferred_element_type=F32)
            u_all = nt_dot(ds, wd[c:c + 256, :])
            grads = []
            for i in range(g):
                act = act_all[i * hi:i * hi + rows]
                u = u_all[i * span + off:i * span + off + rows]
                sig = jax.nn.sigmoid(act)
                hid = (act * sig).astype(BF16).astype(F32)
                terms[i] = terms[i] + jnp.sum(hid * u, axis=1, keepdims=True)
                grads.append(u * sig * (1.0 + act * (1.0 - sig)))
            agr[0:g * rows, c:c + 256] = jnp.concatenate(grads, axis=0).astype(BF16)
        for i, j in enumerate(group):
            line = jnp.sum(jnp.where(diag, terms[i], 0.0), axis=0, keepdims=True)
            line = jnp.broadcast_to(line, (8, 128))
            if j == 0:
                grecv[0] = line
            else:
                gsend[j] = line
                copy = remote(gsend, grecv, g_send, g_recv, j)
                copy.start()
                gate_copies.append(copy)
        grad_in = agr[0:g * rows, :]
        left = nt_dot(grad_in, wu[0:half, :])
        right = nt_dot(grad_in, wu[half:width, :])
        for i, j in enumerate(group):
            block = jnp.concatenate(
                [left[i * rows:(i + 1) * rows], right[i * rows:(i + 1) * rows]], axis=0)
            if j == 0:
                rsend[0] = block.astype(BF16)
                own = pltpu.make_async_copy(rsend.at[0], rrecv.at[0], local_sem.at[4])
                own.start()
            else:
                rsend[j] = block.astype(BF16)
                copy = remote(rsend, rrecv, r_send, r_recv, j)
                copy.start()
                back_copies.append(copy)
        for i, j in enumerate(group):
            total = total + jnp.sum(
                recv[j, 0:hi, :].astype(F32)[0:rows] * terms[i], axis=0, keepdims=True)
        if number == 0:
            for h in range(2):
                for j in groups[1]:
                    out_copies[j][h].wait_send()
                for j in groups[2]:
                    out_copies[j][h].start()

    cols[my_dp] = total
    col_copies = []
    for k in range(1, dp):
        copy = pltpu.make_async_remote_copy(
            src_ref=cols.at[my_dp], dst_ref=cols.at[my_dp], send_sem=c_send.at[k],
            recv_sem=c_recv.at[k], device_id=(lax.rem(my_dp + k, dp), me), device_id_type=MESH)
        copy.start()
        col_copies.append(copy)

    for copy in gate_copies:
        copy.wait_recv()
    gate_out = jnp.zeros(ids.shape, F32)
    for j in range(n):
        col = jnp.sum(jnp.where(diag, grecv[j, 0:1, :], 0.0), axis=1, keepdims=True)
        term = jnp.sum(pick[j * rows:(j + 1) * rows, :] * col, axis=0, keepdims=True)
        gate_out = gate_out + jnp.where(ids == EXP_DEV * peers[j], term, 0.0)
    gg_ref[...] = gate_out

    for k in range(1, dp):
        src = lax.rem(my_dp + dp - k, dp)
        pltpu.make_async_remote_copy(
            src_ref=cols.at[src], dst_ref=cols.at[src], send_sem=c_send.at[k],
            recv_sem=c_recv.at[k], device_id=(src, me), device_id_type=MESH).wait_recv()
    col = cols[0]
    for i in range(1, dp):
        col = col + cols[i]
    rg_ref[...] = col / F32(tok_count * dp)

    for j in groups[2]:
        for copy in out_copies[j]:
            copy.wait_send()
    own.wait()
    for copy in gate_copies + back_copies + col_copies:
        copy.wait_send()
    for copy in back_copies:
        copy.wait_recv()


def combine(n, rows, back, gl, gr, gg_in, rg_in, tg_ref, gg_ref, rg_ref):
    half = back.shape[2]
    hi = -(-rows // 16) * 16
    lo = rows // 16 * 16
    back_l = jnp.concatenate([back[j, 0:hi, :] for j in range(n)], axis=0)
    tg_ref[:, 0:half] = jnp.dot(gl[...], back_l, preferred_element_type=F32).astype(BF16)
    back_r = jnp.concatenate([back[j, lo:2 * rows, :] for j in range(n)], axis=0)
    tg_ref[:, half:2 * half] = jnp.dot(gr[...], back_r, preferred_element_type=F32).astype(BF16)
    gg_ref[...] = gg_in[...].astype(BF16)
    rg_ref[...] = rg_in[...]


def body(tokens, upstream, expert_ids, gate_weights, w_up, w_down):
    n = lax.axis_size("expert")
    dp = lax.axis_size("dp")
    tok_count, width = tokens.shape
    top = expert_ids.shape[1]
    hidden = w_up.shape[2]
    experts = EXP_DEV * n
    most = tok_count * top // experts + tok_count * top // (4 * experts)
    rows = -(-most // 8) * 8
    hi = -(-rows // 16) * 16
    span = 2 * rows - rows // 16 * 16
    groups = [(0,), tuple(range(1, n // 2 + 1)), tuple(range(n // 2 + 1, n))]
    biggest = max(len(g) for g in groups)
    hbm = pl.BlockSpec(memory_space=pltpu.HBM)
    vmem = pl.BlockSpec(memory_space=pltpu.VMEM)
    dma = pltpu.SemaphoreType.DMA
    back, gl, gr, gg, rg = pl.pallas_call(
        functools.partial(kernel, n, dp, rows, groups),
        out_shape=(
            jax.ShapeDtypeStruct((n, 2 * rows, width // 2), BF16),
            jax.ShapeDtypeStruct((tok_count, n * hi), BF16),
            jax.ShapeDtypeStruct((tok_count, n * span), BF16),
            jax.ShapeDtypeStruct((top, tok_count), F32),
            jax.ShapeDtypeStruct((1, width), F32),
        ),
        in_specs=[hbm, hbm, vmem, vmem, hbm, hbm],
        out_specs=(hbm,) + (vmem,) * 4,
        scratch_shapes=[
            pltpu.VMEM((tok_count, width), BF16),
            pltpu.VMEM((tok_count, width), BF16),
            pltpu.VMEM((width, hidden), BF16),
            pltpu.VMEM((hidden, width), BF16),
            pltpu.VMEM((n, 2 * rows, width), BF16),
            pltpu.VMEM((n, 2 * rows, width), BF16),
            pltpu.VMEM((n, 2 * rows, width // 2), BF16),
            pltpu.VMEM((n, 8, 128), F32),
            pltpu.VMEM((n, 8, 128), F32),
            pltpu.VMEM((-(-biggest * rows // 16) * 16, hidden), BF16),
            pltpu.VMEM((dp, 1, width), F32),
            pltpu.VMEM((n * rows, tok_count), F32),
            dma((5,)),
            dma((2 * n,)), dma((2 * n,)), dma((n,)), dma((n,)), dma((n,)), dma((n,)),
            dma((dp,)), dma((dp,)),
        ],
        compiler_params=pltpu.CompilerParams(
            collective_id=0, has_side_effects=True, vmem_limit_bytes=60 * 1024 * 1024),
        cost_estimate=pl.CostEstimate(
            flops=6 * n * rows * width * hidden, bytes_accessed=4 * width * hidden,
            transcendentals=n * rows * hidden),
    )(tokens, upstream, expert_ids.T, gate_weights.T, w_up[0], w_down[0])
    token_grads, gate_t, router = pl.pallas_call(
        functools.partial(combine, n, rows),
        out_shape=(
            jax.ShapeDtypeStruct((tok_count, width), BF16),
            jax.ShapeDtypeStruct((top, tok_count), BF16),
            jax.ShapeDtypeStruct((1, width), F32),
        ),
        in_specs=[vmem] * 5,
        out_specs=(vmem,) * 3,
        compiler_params=pltpu.CompilerParams(vmem_limit_bytes=60 * 1024 * 1024),
    )(back, gl, gr, gg, rg)
    return token_grads, gate_t.T, router


def solution(mesh):
    return jax.shard_map(
        body,
        mesh=mesh,
        in_specs=(
            P(("dp", "expert"), None),
            P(("dp", "expert"), None),
            P(("dp", "expert"), None),
            P(("dp", "expert"), None),
            P("expert", None, None),
            P("expert", None, None),
        ),
        out_specs=(P(("dp", "expert"), None), P(("dp", "expert"), None), P("expert", None)),
        check_vma=False,
    )
```

```python
import functools
import jax
import jax.numpy as jnp
from jax import lax
from jax.experimental import pallas as pl
from jax.experimental.pallas import tpu as pltpu
from jax.sharding import PartitionSpec as P

EXP_DEV = 8
MESH = pl.DeviceIdType.MESH
F32 = jnp.float32
BF16 = jnp.bfloat16


def nt_dot(a, b):
    return lax.dot_general(a, b, (((1,), (1,)), ((), ())), preferred_element_type=F32)


def flipped(me, j):
    out, bit = me, 1
    while bit <= j:
        if (j // bit) % 2:
            out = out + bit - 2 * bit * ((me // bit) % 2)
        bit *= 2
    return out


def kernel(n, dp, rows, groups, tok_hbm, dy_hbm, ids_ref, gate_ref, wu_hbm, wd_hbm,
           rrecv, gl, gr, gg_ref, rg_ref,
           tok, dy, wu, wd, send, recv, rsend, gsend, grecv, agr, cols, pick,
           local_sem, s_send, s_recv, r_send, r_recv, g_send, g_recv, c_send, c_recv):
    me = lax.axis_index("expert")
    my_dp = lax.axis_index("dp")
    tok_count, width = tok.shape
    hidden = wu.shape[1]
    half = width // 2
    hi = -(-rows // 16) * 16
    lo = rows // 16 * 16
    off = rows - lo
    span = 2 * rows - lo
    peers = [flipped(me, j) for j in range(n)]

    loads = [
        pltpu.make_async_copy(src, dst, local_sem.at[i])
        for i, (src, dst) in enumerate(
            ((tok_hbm, tok), (dy_hbm, dy), (wu_hbm, wu), (wd_hbm, wd)))
    ]
    loads[0].start()
    loads[1].start()

    barrier = pltpu.get_barrier_semaphore()
    for j in range(1, n):
        pl.semaphore_signal(barrier, inc=1, device_id=(my_dp, peers[j]), device_id_type=MESH)
    for k in range(1, dp):
        pl.semaphore_signal(
            barrier, inc=1, device_id=(lax.rem(my_dp + k, dp), me), device_id_type=MESH)

    ids = ids_ref[...]
    gates = gate_ref[...].astype(F32)
    hits, gate_rows = [], []
    for j in range(n):
        same = ids == EXP_DEV * peers[j]
        hits.append(jnp.sum(jnp.where(same, 1.0, 0.0), axis=0, keepdims=True))
        gate_rows.append(jnp.sum(jnp.where(same, gates, 0.0), axis=0, keepdims=True))
    pad = [jnp.zeros((128 - n, tok_count), F32)]
    hit_t = jnp.concatenate(hits + pad, axis=0)
    gate_t = jnp.concatenate(gate_rows + pad, axis=0)
    t_row = lax.broadcasted_iota(jnp.int32, (tok_count, tok_count), 0)
    t_col = lax.broadcasted_iota(jnp.int32, (tok_count, tok_count), 1)
    above = jnp.where(t_row < t_col, 1.0, 0.0).astype(BF16)
    eye = jnp.where(t_col == t_row, 1.0, 0.0).astype(BF16)
    rank_t = jnp.dot(hit_t.astype(BF16), above, preferred_element_type=F32)
    key_t = jnp.where(hit_t > 0.5, rank_t, -1.0)

    row_id = lax.broadcasted_iota(jnp.int32, (rows, tok_count), 0).astype(F32)
    for j in range(n):
        pick[j * rows:(j + 1) * rows, :] = jnp.where(row_id == key_t[j:j + 1, :], 1.0, 0.0)
    pick_all = pick[...].astype(BF16)

    def remote(src, dst, a_sem, b_sem, j):
        return pltpu.make_async_remote_copy(
            src_ref=src.at[j], dst_ref=dst.at[j], send_sem=a_sem.at[j], recv_sem=b_sem.at[j],
            device_id=(my_dp, peers[j]), device_id_type=MESH)

    def part(j, h):
        cut = (j, slice(None), pl.ds(h * half, half))
        return pltpu.make_async_remote_copy(
            src_ref=send.at[cut], dst_ref=recv.at[cut], send_sem=s_send.at[2 * j + h],
            recv_sem=s_recv.at[2 * j + h], device_id=(my_dp, peers[j]), device_id_type=MESH)

    out_copies = [[part(j, 0), part(j, 1)] if j else [] for j in range(n)]
    loads[0].wait()
    loads[1].wait()
    loads[2].start()
    loads[3].start()
    for h in range(2):
        for c in range(h * half, h * half + half, 512):
            sel_x = jnp.dot(pick_all, tok[:, c:c + 512], preferred_element_type=F32)
            sel_d = jnp.dot(pick_all, dy[:, c:c + 512], preferred_element_type=F32)
            for j in range(n):
                both = jnp.concatenate(
                    [sel_x[j * rows:(j + 1) * rows], sel_d[j * rows:(j + 1) * rows]], axis=0)
                if j == 0:
                    recv[0, :, c:c + 512] = both.astype(BF16)
                else:
                    send[j, :, c:c + 512] = both.astype(BF16)
        if h == 0:
            pl.semaphore_wait(barrier, n - 1 + dp - 1)
        for j in groups[1]:
            out_copies[j][h].start()

    key = lax.dot_general(
        eye, key_t.astype(BF16), (((1,), (1,)), ((), ())), preferred_element_type=F32)
    gsel = lax.dot_general(
        eye, gate_t.astype(BF16), (((1,), (1,)), ((), ())), preferred_element_type=F32)
    lanes = lax.broadcasted_iota(jnp.int32, (1, n * hi), 1).astype(F32)
    mat = jnp.zeros((tok_count, n * hi), F32)
    mat_r = jnp.zeros((tok_count, n * span), F32)
    lanes_r = lax.broadcasted_iota(jnp.int32, (1, n * span), 1).astype(F32)
    for j in range(n):
        there = key[:, j:j + 1] > -0.5
        spot = jnp.where(there, key[:, j:j + 1] + (hi * j), -1.0)
        mat = mat + jnp.where(lanes == spot, gsel[:, j:j + 1], 0.0)
        spot_r = jnp.where(there, key[:, j:j + 1] + (span * j + off), -1.0)
        mat_r = mat_r + jnp.where(lanes_r == spot_r, gsel[:, j:j + 1], 0.0)
    gl[...] = mat.astype(BF16)
    gr[...] = mat_r.astype(BF16)

    diag = (lax.broadcasted_iota(jnp.int32, (rows, 128), 0)
            == lax.broadcasted_iota(jnp.int32, (rows, 128), 1))
    loads[2].wait()
    loads[3].wait()
    for h in range(2):
        for j in groups[1]:
            out_copies[j][h].wait_send()
        for j in groups[2]:
            out_copies[j][h].start()
    total = jnp.zeros((1, width), F32)
    back_copies, gate_copies, col_copies = [], [], []
    for number, group in enumerate(groups):
        for j in group:
            for copy in out_copies[j]:
                copy.wait_recv()
        g = len(group)
        xs = jnp.concatenate([recv[j, 0:hi, :] for j in group], axis=0)
        ds = jnp.concatenate([recv[j, lo:2 * rows, :] for j in group], axis=0)
        terms = [jnp.zeros((rows, 1), F32) for _ in group]
        for c in range(0, hidden, 256):
            act_all = jnp.dot(xs, wu[:, c:c + 256], preferred_element_type=F32)
            u_all = nt_dot(ds, wd[c:c + 256, :])
            grads = []
            for i in range(g):
                act = act_all[i * hi:i * hi + rows]
                u = u_all[i * span + off:i * span + off + rows]
                sig = jax.nn.sigmoid(act)
                hid = (act * sig).astype(BF16).astype(F32)
                terms[i] = terms[i] + jnp.sum(hid * u, axis=1, keepdims=True)
                grads.append(u * sig * (1.0 + act * (1.0 - sig)))
            agr[0:g * rows, c:c + 256] = jnp.concatenate(grads, axis=0).astype(BF16)
        for i, j in enumerate(group):
            line = jnp.sum(jnp.where(diag, terms[i], 0.0), axis=0, keepdims=True)
            line = jnp.broadcast_to(line, (8, 128))
            if j == 0:
                grecv[0] = line
            else:
                gsend[j] = line
                copy = remote(gsend, grecv, g_send, g_recv, j)
                copy.start()
                gate_copies.append(copy)
        for i, j in enumerate(group):
            total = total + jnp.sum(
                recv[j, 0:hi, :].astype(F32)[0:rows] * terms[i], axis=0, keepdims=True)
        if number == len(groups) - 1:
            cols[my_dp] = total
            for k in range(1, dp):
                copy = pltpu.make_async_remote_copy(
                    src_ref=cols.at[my_dp], dst_ref=cols.at[my_dp], send_sem=c_send.at[k],
                    recv_sem=c_recv.at[k], device_id=(lax.rem(my_dp + k, dp), me), device_id_type=MESH)
                copy.start()
                col_copies.append(copy)
        grad_in = agr[0:g * rows, :]
        for q in range(2):
            c = q * (half // 2)
            left = nt_dot(grad_in, wu[c:c + half // 2, :])
            right = nt_dot(grad_in, wu[half + c:half + c + half // 2, :])
            for i, j in enumerate(group):
                block = jnp.concatenate(
                    [left[i * rows:(i + 1) * rows], right[i * rows:(i + 1) * rows]], axis=0)
                rsend[j, :, c:c + half // 2] = block.astype(BF16)
                if j:
                    cut = (j, slice(None), pl.ds(c, half // 2))
                    copy = pltpu.make_async_remote_copy(
                        src_ref=rsend.at[cut], dst_ref=rrecv.at[cut],
                        send_sem=r_send.at[2 * j + q], recv_sem=r_recv.at[2 * j + q],
                        device_id=(my_dp, peers[j]), device_id_type=MESH)
                    copy.start()
                    back_copies.append(copy)
        if number == 0:
            own = pltpu.make_async_copy(rsend.at[0], rrecv.at[0], local_sem.at[4])
            own.start()

    for copy in gate_copies:
        copy.wait_recv()
    gate_out = jnp.zeros(ids.shape, F32)
    for j in range(n):
        col = jnp.sum(jnp.where(diag, grecv[j, 0:1, :], 0.0), axis=1, keepdims=True)
        term = jnp.sum(pick[j * rows:(j + 1) * rows, :] * col, axis=0, keepdims=True)
        gate_out = gate_out + jnp.where(ids == EXP_DEV * peers[j], term, 0.0)
    gg_ref[...] = gate_out

    for k in range(1, dp):
        src = lax.rem(my_dp + dp - k, dp)
        pltpu.make_async_remote_copy(
            src_ref=cols.at[src], dst_ref=cols.at[src], send_sem=c_send.at[k],
            recv_sem=c_recv.at[k], device_id=(src, me), device_id_type=MESH).wait_recv()
    col = cols[0]
    for i in range(1, dp):
        col = col + cols[i]
    rg_ref[...] = col / F32(tok_count * dp)

    for j in groups[2]:
        for copy in out_copies[j]:
            copy.wait_send()
    own.wait()
    for copy in gate_copies + back_copies + col_copies:
        copy.wait_send()
    for copy in back_copies:
        copy.wait_recv()


def combine(n, rows, back, gl, gr, gg_in, rg_in, tg_ref, gg_ref, rg_ref):
    half = back.shape[2]
    hi = -(-rows // 16) * 16
    lo = rows // 16 * 16
    back_l = jnp.concatenate([back[j, 0:hi, :] for j in range(n)], axis=0)
    tg_ref[:, 0:half] = jnp.dot(gl[...], back_l, preferred_element_type=F32).astype(BF16)
    back_r = jnp.concatenate([back[j, lo:2 * rows, :] for j in range(n)], axis=0)
    tg_ref[:, half:2 * half] = jnp.dot(gr[...], back_r, preferred_element_type=F32).astype(BF16)
    gg_ref[...] = gg_in[...].astype(BF16)
    rg_ref[...] = rg_in[...]


def body(tokens, upstream, expert_ids, gate_weights, w_up, w_down):
    n = lax.axis_size("expert")
    dp = lax.axis_size("dp")
    tok_count, width = tokens.shape
    top = expert_ids.shape[1]
    hidden = w_up.shape[2]
    experts = EXP_DEV * n
    most = tok_count * top // experts + tok_count * top // (4 * experts)
    rows = -(-most // 8) * 8
    hi = -(-rows // 16) * 16
    span = 2 * rows - rows // 16 * 16
    groups = [(0,), tuple(range(1, n // 2 + 1)), tuple(range(n // 2 + 1, n))]
    biggest = max(len(g) for g in groups)
    hbm = pl.BlockSpec(memory_space=pltpu.HBM)
    vmem = pl.BlockSpec(memory_space=pltpu.VMEM)
    dma = pltpu.SemaphoreType.DMA
    back, gl, gr, gg, rg = pl.pallas_call(
        functools.partial(kernel, n, dp, rows, groups),
        out_shape=(
            jax.ShapeDtypeStruct((n, 2 * rows, width // 2), BF16),
            jax.ShapeDtypeStruct((tok_count, n * hi), BF16),
            jax.ShapeDtypeStruct((tok_count, n * span), BF16),
            jax.ShapeDtypeStruct((top, tok_count), F32),
            jax.ShapeDtypeStruct((1, width), F32),
        ),
        in_specs=[hbm, hbm, vmem, vmem, hbm, hbm],
        out_specs=(hbm,) + (vmem,) * 4,
        scratch_shapes=[
            pltpu.VMEM((tok_count, width), BF16),
            pltpu.VMEM((tok_count, width), BF16),
            pltpu.VMEM((width, hidden), BF16),
            pltpu.VMEM((hidden, width), BF16),
            pltpu.VMEM((n, 2 * rows, width), BF16),
            pltpu.VMEM((n, 2 * rows, width), BF16),
            pltpu.VMEM((n, 2 * rows, width // 2), BF16),
            pltpu.VMEM((n, 8, 128), F32),
            pltpu.VMEM((n, 8, 128), F32),
            pltpu.VMEM((-(-biggest * rows // 16) * 16, hidden), BF16),
            pltpu.VMEM((dp, 1, width), F32),
            pltpu.VMEM((n * rows, tok_count), F32),
            dma((5,)),
            dma((2 * n,)), dma((2 * n,)), dma((2 * n,)), dma((2 * n,)), dma((n,)), dma((n,)),
            dma((dp,)), dma((dp,)),
        ],
        compiler_params=pltpu.CompilerParams(
            collective_id=0, has_side_effects=True, vmem_limit_bytes=60 * 1024 * 1024),
        cost_estimate=pl.CostEstimate(
            flops=6 * n * rows * width * hidden, bytes_accessed=4 * width * hidden,
            transcendentals=n * rows * hidden),
    )(tokens, upstream, expert_ids.T, gate_weights.T, w_up[0], w_down[0])
    token_grads, gate_t, router = pl.pallas_call(
        functools.partial(combine, n, rows),
        out_shape=(
            jax.ShapeDtypeStruct((tok_count, width), BF16),
            jax.ShapeDtypeStruct((top, tok_count), BF16),
            jax.ShapeDtypeStruct((1, width), F32),
        ),
        in_specs=[vmem] * 5,
        out_specs=(vmem,) * 3,
        compiler_params=pltpu.CompilerParams(vmem_limit_bytes=60 * 1024 * 1024),
    )(back, gl, gr, gg, rg)
    return token_grads, gate_t.T, router


def solution(mesh):
    return jax.shard_map(
        body,
        mesh=mesh,
        in_specs=(
            P(("dp", "expert"), None),
            P(("dp", "expert"), None),
            P(("dp", "expert"), None),
            P(("dp", "expert"), None),
            P("expert", None, None),
            P("expert", None, None),
        ),
        out_specs=(P(("dp", "expert"), None), P(("dp", "expert"), None), P("expert", None)),
        check_vma=False,
    )
```
